256 devices in a mesh: slab: 32 (over z, y_lo, core), harm: 8 (over x, y_hi).
Axes of the slice: x: 4, y: 4 (y_hi: 2, y_lo: 2; y = y_hi * 2 + y_lo), z: 8, core: 2. Of those that a mesh axis runs over, the one named last changes fastest.
Arguments:
- adjoint: float32 [64, 3, 32, 128, 128], P('harm', None, 'slab'), may hold values from -6 to 6
- jacobian: bfloat16 [3, 3, 128, 32, 128, 128], P(None, None, None, 'slab', 'harm'), may hold values from -0.9 to 6, as said below
- conductivity: float32 [32, 128, 128], P('slab'), may hold values from 0.2 to 2
- harm_order: int32 [32], replicated, may hold values from 1 to 63, as said below
Outputs:
- first_image: float32 [64, 3, 32, 128, 128], P('harm', None, 'slab')
- second_image: float32 [64, 3, 32, 128, 128], P('harm', None, 'slab')
The draws below stay inside these ranges and needn't reach their ends.
Inputs may be any that keep to these rules, and one draw needn't show every extreme that they name: `jacobian`: saved reluctivity Jacobians, three by three for each time sample and cell. `harm_order`: each of the first 32 odd numbers once.
All inputs are finite; a program needn't handle non-finite values.
Results may differ from the reference program's by a relative error of at most 0.0086.
Values may be sent and summed in bfloat16 or wider, within the bound.
A program may use at most 64 MiB of HBM per device.

```python
import math
import jax
import jax.numpy as jnp
from jax import lax

H = 32
NT = 128
NX = 128
NY = 128
C = 64
NZ = 32


def draw_jacobian(key, part):
    key = jax.random.fold_in(key, 1)
    key_off = jax.random.fold_in(key, 11)
    key_diag = jax.random.fold_in(key, 12)
    shape = (3, 3, NT, NZ, NX, NY)
    off_diag = jax.random.uniform(key_off, shape, jnp.float32, -0.6, 0.6)
    diag = jnp.exp(jax.random.uniform(key_diag, shape, jnp.float32, 0.0, 1.3862944))
    rows = jnp.arange(3, dtype=jnp.int32)
    unit = (rows[:, None] == rows[None, :]).astype(jnp.float32).reshape(3, 3, 1, 1, 1, 1)
    return (off_diag * (1.0 - unit) + diag * unit).astype(jnp.bfloat16)


def draw_harm_order(key, part):
    key = jax.random.fold_in(key, 2)
    return (2 * jax.random.permutation(key, H) + 1).astype(jnp.int32)


def block_scale(stream_key, extent, split, smallest, largest):
    def one(axis_at, parts):
        heights = jax.random.uniform(jax.random.fold_in(jax.random.fold_in(stream_key, 6), axis_at), (parts,), jnp.float32, smallest / len(split), largest / len(split))
        return jnp.repeat(jnp.exp(heights), extent[axis_at] // parts).reshape((-1,) + (1,) * (len(extent) - axis_at - 1))

    gain = one(*split[0])
    for cut in split[1:]:
        gain = gain * one(*cut)
    return gain


def normal_values(own_key, extent, spread, bound, split=(), kind=jnp.bfloat16):
    array = spread * jax.random.normal(own_key, extent, jnp.float32)
    if split:
        array = array * block_scale(own_key, extent, split, -0.22, 0.18)
    return jnp.clip(array, -bound, bound).astype(kind)


def setup_inputs(seed: int = 0) -> dict:
    streams_of = jax.random.split(jax.random.key(seed), 5)
    return {
        "adjoint": normal_values(streams_of[0], (C, 3, NZ, NX, NY), 1.0, 6.0, ((0, 8), (2, 32)), jnp.float32),
        "jacobian": draw_jacobian(jax.random.fold_in(streams_of[4], 71), 0),
        "conductivity": jnp.clip(jnp.exp(math.log(2.0) - 2.3025851 * jax.random.uniform(streams_of[2], (NZ, NX, NY), jnp.float32) ** block_scale(streams_of[2], (NZ, NX, NY), ((0, 32),), -0.2, 0.2)), 0.2, 2.0),
        "harm_order": draw_harm_order(jax.random.fold_in(streams_of[4], 71), 0),
    }


def build_table(harm_order, steps):
    sample_ids = jnp.arange(steps, dtype=jnp.int32)
    phases = (harm_order[:, None] * sample_ids[None, :]) % steps
    angles = phases.astype(jnp.float32) * (2.0 * math.pi / steps)
    paired = jnp.stack([jnp.cos(angles), jnp.sin(angles)], axis=1)
    return paired.reshape(-1, steps).astype(jnp.bfloat16)


def reluct_part(packed, jacobian, table):
    coeff_count = table.shape[0]

    def per_plane(plane):
        coeff_plane = lax.dynamic_index_in_dim(packed, plane, 2, keepdims=False)
        jac_plane = lax.dynamic_index_in_dim(jacobian, plane, 3, keepdims=False)
        samples = jnp.dot(table.T, coeff_plane.reshape(coeff_count, -1), preferred_element_type=jnp.float32)
        samples = samples.astype(jnp.bfloat16).reshape((NT, 3) + coeff_plane.shape[2:])
        weighted = []
        for comp_out in range(3):
            total = jnp.zeros(samples[:, 0].shape, jnp.float32)
            for comp_in in range(3):
                total = total + jac_plane[comp_in, comp_out].astype(jnp.float32) * samples[:, comp_in].astype(jnp.float32)
            weighted.append(total)
        weighted = jnp.stack(weighted, axis=1).astype(jnp.bfloat16)
        coeffs = jnp.dot(table, weighted.reshape(NT, -1), preferred_element_type=jnp.float32) * (2.0 / NT)
        return coeffs.astype(jnp.bfloat16).reshape(coeff_plane.shape)

    planes_out = lax.map(per_plane, jnp.arange(packed.shape[2], dtype=jnp.int32))
    return jnp.moveaxis(planes_out, 0, 2)


def transposed_apply(adjoint_in, jacobian, conductivity, harm_order, table):
    packed = adjoint_in.astype(jnp.bfloat16)
    coeffs = reluct_part(packed, jacobian, table).astype(jnp.float32)
    padded = jnp.pad(coeffs, ((0, 0), (0, 0), (1, 1), (1, 1), (1, 1)))
    beside = padded[:, :, 2:, 1:-1, 1:-1] + padded[:, :, :-2, 1:-1, 1:-1]
    beside = beside + padded[:, :, 1:-1, 2:, 1:-1] + padded[:, :, 1:-1, :-2, 1:-1]
    beside = beside + padded[:, :, 1:-1, 1:-1, 2:] + padded[:, :, 1:-1, 1:-1, :-2]
    orders = harm_order.astype(jnp.float32) / (2.0 * H)
    paired = adjoint_in.reshape((H, 2) + adjoint_in.shape[1:])
    factor = orders.reshape(-1, 1, 1, 1, 1) * conductivity[None, None]
    eddy_term = jnp.stack([factor * paired[:, 1], -factor * paired[:, 0]], axis=1).reshape(adjoint_in.shape)
    return 0.25 * (6.0 * coeffs - beside) + eddy_term


def reference(adjoint, jacobian, conductivity, harm_order):
    table = build_table(harm_order, NT)
    first_image = transposed_apply(adjoint, jacobian, conductivity, harm_order, table)
    second_image = transposed_apply(first_image, jacobian, conductivity, harm_order, table)
    return first_image, second_image
```

```python
import math

import jax
import jax.numpy as jnp
from jax import lax
from jax.experimental import pallas as pl
from jax.experimental.pallas import tpu as pltpu
from jax.sharding import PartitionSpec as P

H = 32
NT = 128
HALF = NT // 2
C = 2 * H
R = 8
K = C * R
MESH = pl.DeviceIdType.MESH
F32 = jnp.float32
BF16 = jnp.bfloat16


def kernel(
    adj_hbm, jac_hbm, cond_hbm, orders_hbm,
    out1, out2,
    adj, cond, orders, mat, pk, x1, jac, jeff, tf, tb, wgt, cf, c1, zm, zo, xs, xr, x2, r1, e1, m1, c2, r2, e2, m2,
    fac1, fac2, my, ms, mc, mh, mf,
    jsem, adj_sem, cond_sem, ord_sem, a_s, a_r, z_s, z_r, x_s, x_r, f_s, f_r, o_s, o_r, e_s, e_r, m_s, m_r,
    fa_s, fa_r, fc_s, fc_r, n_s, n_r,
):
    p = lax.axis_index("slab")
    h = lax.axis_index("harm")
    planes = lax.axis_size("slab")
    n = lax.axis_size("harm")
    odd = lax.rem(p, 2)
    mate = p + 1 - 2 * odd
    outer = p - 1 + 2 * odd
    has_outer = jnp.logical_and(outer >= 0, outer < planes)

    def peer(k):
        return lax.rem(h + k, n)

    def rdma(src, dst, ss, rs, dev):
        return pltpu.make_async_remote_copy(
            src_ref=src, dst_ref=dst, send_sem=ss, recv_sem=rs, device_id=dev, device_id_type=MESH
        )

    def adj_copy(q):
        part = pl.ds(2 * q, 2)
        return pltpu.make_async_copy(adj_hbm.at[part], adj.at[part], adj_sem.at[q])

    for q in range(4):
        adj_copy(q).start()
    ord_copy = pltpu.make_async_copy(orders_hbm, orders, ord_sem)
    ord_copy.start()
    cond_copy = pltpu.make_async_copy(cond_hbm, cond, cond_sem)
    cond_copy.start()
    jcopy = pltpu.make_async_copy(jac_hbm, jac, jsem)
    jcopy.start()

    hx, hy = h // 2, lax.rem(h, 2)

    def at(dx, y):
        return 2 * lax.rem(hx + dx + 4, 4) + y

    def flip_dst(dx):
        return at(dx, 1 - hy)

    DIRECT = (2, 1, 3)
    FLIPS = (2, 1, 3, 0)

    barrier = pltpu.get_barrier_semaphore()
    for k in range(1, n):
        pl.semaphore_signal(barrier, inc=1, device_id=(p, peer(k)), device_id_type=MESH)
    pl.semaphore_signal(barrier, inc=1, device_id=(mate, h), device_id_type=MESH)

    @pl.when(has_outer)
    def _():
        for k in range(n):
            pl.semaphore_signal(barrier, inc=1, device_id=(outer, peer(k)), device_id_type=MESH)

    for q in range(4):
        adj_copy(q).wait()

        def pack(g, _, q=q):
            rows = pl.ds(pl.multiple_of(g * R, R), R)
            for i in range(3):
                both = jnp.concatenate([adj[2 * q, i, 0, rows, :], adj[2 * q + 1, i, 0, rows, :]], axis=0)
                pk[g, i, q] = both.astype(BF16)
            return 0

        lax.fori_loop(0, 2 * n, pack, 0, unroll=4)

    pl.semaphore_wait(barrier, n + n * has_outer.astype(jnp.int32))

    def a2a(g, dx):
        dst = at(dx, hy)
        return rdma(pk.at[2 * dst + g], x1.at[g, :, pl.ds(4 * h, 4)], a_s.at[g, dx], a_r.at[g, dx], (p, dst))

    def a2a_flip(g, dx):
        dst = flip_dst(dx)
        return rdma(pk.at[2 * dst + g], x1.at[g, :, pl.ds(4 * h, 4)], fa_s.at[g, dx], fa_r.at[g, dx], (p, dst))

    for g in range(2):
        for dx in FLIPS:
            a2a_flip(g, dx).start()
        for dx in DIRECT:
            a2a(g, dx).start()

    for g in range(2):
        x1[g, :, pl.ds(4 * h, 4)] = pk[2 * h + g]

    ord_copy.wait()
    for k in range(H):
        mat[2 * k:2 * k + 2, :] = jnp.full((2, 128), orders[k], jnp.int32)
    steps = lax.broadcasted_iota(jnp.int32, (C, 128), 1)
    quarter = (lax.broadcasted_iota(jnp.int32, (C, 128), 0) & 1) * (NT // 4)
    phases = (mat[...] * steps + (NT - quarter)) & (NT - 1)
    tab = jnp.cos(phases.astype(F32) * (2.0 * math.pi / NT))[:, :HALF].astype(BF16)

    def iota(shape, dim):
        return lax.broadcasted_iota(jnp.int32, shape, dim)

    def spread(dims, dst):
        cols = ((iota((C, K), 1) >> 3) == iota((C, K), 0)).astype(F32).astype(BF16)
        rows = ((iota((K, C), 0) >> 3) == iota((K, C), 1)).astype(F32).astype(BF16)
        mid = lax.dot_general(rows, tab, dims, preferred_element_type=F32).astype(BF16)
        full = jnp.dot(mid, cols, preferred_element_type=F32)
        same = ((iota((K, K), 0) ^ iota((K, K), 1)) & (R - 1)) == 0
        dst[...] = jnp.where(same, full, 0.0).astype(BF16)

    spread((((1,), (1,)), ((), ())), tf)
    spread((((1,), (0,)), ((), ())), tb)


    QUARTER = 0.25

    def fill(dst, *terms):
        total = jnp.zeros(dst.shape, F32)
        for where, value in terms:
            total = jnp.where(where, value, total)
        dst[...] = total.astype(BF16)

    ya, yb = iota((128, 128), 0), iota((128, 128), 1)
    fill(my, (ya == yb, 6.0 * QUARTER), (jnp.abs(ya - yb) == 1, -QUARTER))
    sa, sb = iota((256, 256), 0), iota((256, 256), 1)
    alike = (sa >> 3) == (sb >> 3)
    fill(ms, (jnp.logical_and(alike, jnp.abs(sa - sb) == 1), -QUARTER))
    fill(mc.at[0], (jnp.logical_and(alike, sa - sb == R - 1), -QUARTER))
    fill(mc.at[1], (jnp.logical_and(alike, sb - sa == R - 1), -QUARTER))
    ha, hb = iota((256, 32), 0), iota((256, 32), 1)
    fill(mh.at[0], (ha == hb * R, -QUARTER))
    fill(mh.at[1], (ha == hb * R + R - 1, -QUARTER))
    down = sb - sa
    step_down = jnp.where((sa & (R - 1)) == R - 1, R + 1, 1)
    step_up = jnp.where((sa & (R - 1)) == 0, -(R + 1), -1)
    fill(mf, (down == step_down, -QUARTER), (down == step_up, -QUARTER))

    cond_copy.wait()
    for g in range(2):
        cnd = cond[0, pl.ds(pl.multiple_of(2 * R * h + g * R, R), R), :]
        for q in range(H):
            fac1[g, q, 0] = orders[q].astype(F32) * (1.0 / (2.0 * H)) * cnd
    for q in range(4):
        fac2[q] = (orders[4 * h + q].astype(F32) * (1.0 / (2.0 * H)) * cond[0]).reshape(2 * n, 1, R, 128)

    jcopy.wait()
    for a in range(3):
        for b in range(3):

            def fold(t, _, a=a, b=b):
                both = jac[a, b, t, 0].astype(F32) + jac[a, b, t + HALF, 0].astype(F32)
                both = both * (2.0 / NT)
                rows = pl.ds(pl.multiple_of(t * R, R), R)
                jeff[0, a, b, rows, :] = both[:R]
                jeff[1, a, b, rows, :] = both[R:]
                return 0

            lax.fori_loop(0, HALF, fold, 0, unroll=8)

    MB = 256

    def forward(src, g):
        cells = jnp.concatenate([src[g, i].reshape(K, 128) for i in range(3)], axis=1)

        def body(m, _):
            rows = pl.ds(pl.multiple_of(m * MB, MB), MB)
            smp = jnp.dot(tf[rows, :], cells, preferred_element_type=F32)
            for b in range(3):
                total = jeff[g, 0, b, rows, :] * smp[:, :128]
                total = total + jeff[g, 1, b, rows, :] * smp[:, 128:256]
                total = total + jeff[g, 2, b, rows, :] * smp[:, 256:]
                wgt[g, rows, 128 * b:128 * b + 128] = total.astype(BF16)
            return 0

        lax.fori_loop(0, K // MB, body, 0)

    def backward(g, dst, keep):
        def body(m, _):
            rows = pl.ds(pl.multiple_of(m * MB, MB), MB)
            pairs = pl.ds(m * (MB // R // 2), MB // R // 2)
            coef = jnp.dot(tb[rows, :], wgt[g], preferred_element_type=F32)
            for i in range(3):
                part = coef[:, 128 * i:128 * i + 128]
                if keep:
                    cf[i, rows, :] = part
                dst[g, i, pairs] = part.astype(BF16).reshape(MB // R // 2, 2 * R, 128)
            return 0

        lax.fori_loop(0, K // MB, body, 0)

    def xhalo(d, dst):
        return rdma(xs.at[d], xr.at[d], x_s.at[d], x_r.at[d], (p, dst))

    def zsend(g, i, d):
        if d == 0:
            return rdma(c1.at[g, i], zm.at[g, i], z_s.at[0, g, i], z_r.at[0, g, i], (mate, h))
        return rdma(c1.at[g, i], zo.at[g, i], z_s.at[1, g, i], z_r.at[1, g, i], (outer, h))

    def feed(kind, g, dx):
        dst = at(dx, hy) if kind < 2 else flip_dst(dx)
        src = (c1, zo, zo, c1)[kind]
        to = r1 if kind in (0, 2) else e1
        return rdma(
            src.at[g, :, pl.ds(4 * dst, 4)], to.at[2 * h + g], f_s.at[kind, g, dx], f_r.at[kind, g, dx],
            (p if kind < 2 else outer, dst),
        )

    def feed_end(g, dx):
        dst = flip_dst(dx)
        return rdma(
            c1.at[g, :, pl.ds(4 * dst, 4)], r1.at[2 * h + g], f_s.at[2, g, dx], f_r.at[2, g, dx], (p, dst)
        )

    for g in range(2):
        for dx in DIRECT:
            a2a(g, dx).wait_recv()
        for dx in FLIPS:
            a2a_flip(g, dx).wait_recv()
        forward(x1, g)
        backward(g, c1, True)

        @pl.when(has_outer)
        def _():
            for i in range(3):
                zsend(g, i, 1).start()

        for i in range(3):
            zsend(g, i, 0).start()

        for i in range(3):
            xs[g, i] = cf[i, pl.ds(0 if g == 0 else R - 1, C, stride=R), :].astype(BF16)

        if g == 0:

            @pl.when(h > 0)
            def _():
                xhalo(0, h - 1).start()

        else:

            @pl.when(h < n - 1)
            def _():
                xhalo(1, h + 1).start()

        @pl.when(has_outer)
        def _():
            for dx in range(4):
                feed(3, g, dx).start()

        @pl.when(jnp.logical_not(has_outer))
        def _():
            for dx in range(4):
                feed_end(g, dx).start()

        for dx in DIRECT:
            feed(0, g, dx).start()
        r1[2 * h + g] = c1[g, :, pl.ds(4 * h, 4)]

    def swapped(v, factor):
        return jnp.concatenate([factor * v[:, 1:], -(factor * v[:, :1])], axis=1)

    for g in range(2):
        has_x = h > 0 if g == 0 else h < n - 1

        @pl.when(has_x)
        def _():
            xhalo(1 - g, h).wait_recv()

        @pl.when(jnp.logical_not(has_x))
        def _():
            xr[1 - g] = jnp.zeros_like(xr[1 - g])

        for i in range(3):

            @pl.when(has_outer)
            def _():
                zsend(g, i, 1).wait_recv()

            @pl.when(jnp.logical_not(has_outer))
            def _():
                zo[g, i] = jnp.zeros_like(zo[g, i])

            zsend(g, i, 0).wait_recv()

            def first(b, _, g=g, i=i):
                pairs = pl.ds(16 * b, 16)
                mine = c1[g, i, pairs].reshape(256, 128)
                other = c1[1 - g, i, pairs].reshape(256, 128)
                halo = xr[1 - g, i, pl.ds(pl.multiple_of(32 * b, 32), 32), :]
                total = jnp.dot(mine, my[...], preferred_element_type=F32)
                total = total + jnp.dot(ms[...], mine, preferred_element_type=F32)
                total = total + jnp.dot(mc[g], other, preferred_element_type=F32)
                total = total + jnp.dot(mh[g], halo, preferred_element_type=F32)
                axial = zm[g, i, pairs].astype(F32) + zo[g, i, pairs].astype(F32)
                eddy = swapped(x1[g, i, pairs].astype(F32).reshape(16, 2, R, 128), fac1[g, pairs])
                total = total.reshape(16, 2 * R, 128) - QUARTER * axial + eddy.reshape(16, 2 * R, 128)
                x2[g, i, pairs] = total.astype(BF16)
                return 0

            lax.fori_loop(0, 2, first, 0)

        @pl.when(has_outer)
        def _():
            for dx in range(4):
                feed(2, g, dx).start()
            for dx in DIRECT:
                feed(1, g, dx).start()
            e1[2 * h + g] = zo[g, :, pl.ds(4 * h, 4)]

        @pl.when(jnp.logical_not(has_outer))
        def _():
            for k in range(n):
                e1[2 * k + g] = jnp.zeros_like(e1[2 * k + g])

        forward(x2, g)
        backward(g, c2, False)

    def own(i, dx):
        dst = at(dx, hy)
        return rdma(
            c2.at[:, i, pl.ds(4 * dst, 4)], r2.at[pl.ds(2 * h, 2), i], o_s.at[i, dx], o_r.at[i, dx], (p, dst)
        )

    def own_flip(i, dx):
        dst = flip_dst(dx)
        return rdma(
            c2.at[:, i, pl.ds(4 * dst, 4)], r2.at[pl.ds(2 * h, 2), i], fc_s.at[i, dx], fc_r.at[i, dx], (p, dst)
        )

    def edge(i, k):
        dst = peer(k)
        return rdma(
            c2.at[:, i, pl.ds(4 * dst, 4)], e2.at[pl.ds(2 * h, 2), i], e_s.at[i, k], e_r.at[i, k], (outer, dst)
        )

    def to_mate(i):
        return rdma(r2.at[:, i], m2.at[:, i], m_s.at[i], m_r.at[i], (mate, h))

    for i in range(3):
        for dx in FLIPS:
            own_flip(i, dx).start()
        for dx in DIRECT:
            own(i, dx).start()

        @pl.when(has_outer)
        def _():
            for k in (4, 5, 3, 1, 7, 2, 6, 0):
                edge(i, k).start()

    for g in range(2):
        r2[2 * h + g] = c2[g, :, pl.ds(4 * h, 4)]


    def finish(r, e, m, v, out, i):
        for q in range(4):
            mine = r[:, i, q].reshape(256, 128)
            total = jnp.dot(mine, my[...], preferred_element_type=F32)
            total = total + jnp.dot(mf[...], mine, preferred_element_type=F32)
            axial = e[:, i, q].astype(F32) + m[:, i, q].astype(F32)
            total = (total.reshape(2 * n, 2 * R, 128) - QUARTER * axial).reshape(2 * n, 2, R, 128)
            factor = fac2[q].reshape(2 * n * R, 128)
            out[2 * q, i, 0] = total[:, 0].reshape(2 * n * R, 128) + factor * v[2 * q + 1, i, 0]
            out[2 * q + 1, i, 0] = total[:, 1].reshape(2 * n * R, 128) - factor * v[2 * q, i, 0]

    def first_to_mate(i):
        return rdma(r1.at[:, i], m1.at[:, i], n_s.at[i], n_r.at[i], (mate, h))

    for g in range(2):
        for dx in DIRECT:
            feed(0, g, dx).wait_recv()
        for dx in range(4):
            feed_end(g, dx).wait_recv()
    for i in range(3):
        first_to_mate(i).start()

    @pl.when(has_outer)
    def _():
        for g in range(2):
            for dx in DIRECT:
                feed(1, g, dx).wait_recv()
            for dx in range(4):
                feed(3, g, dx).wait_recv()

    for i in range(3):
        first_to_mate(i).wait_recv()
        finish(r1, e1, m1, adj, out1, i)

    def finish_second(i):
        @pl.when(has_outer)
        def _():
            for k in range(n):
                edge(i, k).wait_recv()

        @pl.when(jnp.logical_not(has_outer))
        def _():
            e2[:, i] = jnp.zeros_like(e2[:, i])

        to_mate(i).wait_recv()
        finish(r2, e2, m2, out1, out2, i)

    for i in range(3):
        for dx in DIRECT:
            own(i, dx).wait_recv()
        for dx in FLIPS:
            own_flip(i, dx).wait_recv()
        to_mate(i).start()
        if i > 0:
            finish_second(i - 1)
    finish_second(2)

    for g in range(2):
        for dx in DIRECT:
            a2a(g, dx).wait_send()
            feed(0, g, dx).wait_send()
        for dx in FLIPS:
            a2a_flip(g, dx).wait_send()
        for dx in range(4):
            feed_end(g, dx).wait_send()

        @pl.when(has_outer)
        def _():
            for dx in DIRECT:
                feed(1, g, dx).wait_send()
            for dx in range(4):
                feed(3, g, dx).wait_send()

    @pl.when(h > 0)
    def _():
        xhalo(0, h - 1).wait_send()

    @pl.when(h < n - 1)
    def _():
        xhalo(1, h + 1).wait_send()

    for i in range(3):

        for g in range(2):
            zsend(g, i, 0).wait_send()

        @pl.when(has_outer)
        def _():
            for g in range(2):
                zsend(g, i, 1).wait_send()

        first_to_mate(i).wait_send()
        for dx in DIRECT:
            own(i, dx).wait_send()
        for dx in FLIPS:
            own_flip(i, dx).wait_send()

        @pl.when(has_outer)
        def _():
            for k in range(n):
                edge(i, k).wait_send()

        to_mate(i).wait_send()


def shards(adjoint, jacobian, conductivity, harm_order):
    n = lax.axis_size("harm")
    hbm = pl.BlockSpec(memory_space=pltpu.HBM)
    vmem = pl.BlockSpec(memory_space=pltpu.VMEM)
    pinned = [pltpu.with_memory_space_constraint(v, pltpu.HBM) for v in (adjoint, jacobian, conductivity, harm_order)]
    shape = jax.ShapeDtypeStruct(adjoint.shape, F32)
    by_rows = (2, 3, C // 2, 2 * R, 128)
    by_coeffs = (2 * n, 3, C // 2 // n, 2 * R, 128)
    dma = pltpu.SemaphoreType.DMA
    return pl.pallas_call(
        kernel,
        out_shape=(shape, shape),
        in_specs=[hbm, hbm, hbm, hbm],
        out_specs=(vmem, vmem),
        scratch_shapes=[
            pltpu.VMEM(adjoint.shape, F32),
            pltpu.VMEM(conductivity.shape, F32),
            pltpu.SMEM(harm_order.shape, jnp.int32),
            pltpu.VMEM((C, 128), jnp.int32),
            pltpu.VMEM(by_coeffs, BF16),
            pltpu.VMEM(by_rows, BF16),
            pltpu.VMEM(jacobian.shape, BF16),
            pltpu.VMEM((2, 3, 3, K, 128), F32),
            pltpu.VMEM((K, K), BF16),
            pltpu.VMEM((K, K), BF16),
            pltpu.VMEM((2, K, 3 * 128), BF16),
            pltpu.VMEM((3, K, 128), F32),
            pltpu.VMEM(by_rows, BF16),
            pltpu.VMEM(by_rows, BF16),
            pltpu.VMEM(by_rows, BF16),
            pltpu.VMEM((2, 3, C, 128), BF16),
            pltpu.VMEM((2, 3, C, 128), BF16),
            pltpu.VMEM(by_rows, BF16),
            pltpu.VMEM(by_coeffs, BF16),
            pltpu.VMEM(by_coeffs, BF16),
            pltpu.VMEM(by_coeffs, BF16),
            pltpu.VMEM(by_rows, BF16),
            pltpu.VMEM(by_coeffs, BF16),
            pltpu.VMEM(by_coeffs, BF16),
            pltpu.VMEM(by_coeffs, BF16),
            pltpu.VMEM((2, H, 1, R, 128), F32),
            pltpu.VMEM((4, 2 * n, 1, R, 128), F32),
            pltpu.VMEM((128, 128), BF16),
            pltpu.VMEM((256, 256), BF16),
            pltpu.VMEM((2, 256, 256), BF16),
            pltpu.VMEM((2, 256, 32), BF16),
            pltpu.VMEM((256, 256), BF16),
            dma, dma((4,)), dma, dma,
            dma((2, n)), dma((2, n)),
            dma((2, 2, 3)), dma((2, 2, 3)),
            dma((2,)), dma((2,)),
            dma((4, 2, 4)), dma((4, 2, 4)),
            dma((3, n)), dma((3, n)),
            dma((3, n)), dma((3, n)),
            dma((3,)), dma((3,)),
            dma((2, 4)), dma((2, 4)),
            dma((3, 4)), dma((3, 4)),
            dma((3,)), dma((3,)),
        ],
        compiler_params=pltpu.CompilerParams(
            collective_id=0, has_side_effects=True, vmem_limit_bytes=48 * 1024 * 1024
        ),
    )(*pinned)


def solution(mesh):
    return jax.shard_map(
        shards,
        mesh=mesh,
        in_specs=(
            P("harm", None, "slab", None, None),
            P(None, None, None, "slab", "harm", None),
            P("slab", None, None),
            P(),
        ),
        out_specs=(P("harm", None, "slab", None, None), P("harm", None, "slab", None, None)),
        check_vma=False,
    )
```

```python
import math

import jax
import jax.numpy as jnp
from jax import lax
from jax.experimental import pallas as pl
from jax.experimental.pallas import tpu as pltpu
from jax.sharding import PartitionSpec as P

H = 32
NT = 128
HALF = NT // 2
C = 2 * H
R = 8
K = C * R
MESH = pl.DeviceIdType.MESH
F32 = jnp.float32
BF16 = jnp.bfloat16


def kernel(
    adj_hbm, jac_hbm, cond_hbm, orders_hbm,
    out1, out2,
    adj, cond, orders, mat, pk, x1, jac, jeff, tf, tb, wgt, cf, c1, zm, zo, xs, xr, x2, r1, e1, m1, c2, r2, e2, m2,
    fac1, fac2, my, ms, mc, mh, mf,
    jsem, adj_sem, cond_sem, ord_sem, a_s, a_r, z_s, z_r, x_s, x_r, f_s, f_r, o_s, o_r, e_s, e_r, m_s, m_r,
    fa_s, fa_r, fc_s, fc_r, n_s, n_r,
):
    p = lax.axis_index("slab")
    h = lax.axis_index("harm")
    planes = lax.axis_size("slab")
    n = lax.axis_size("harm")
    odd = lax.rem(p, 2)
    mate = p + 1 - 2 * odd
    outer = lax.rem(p - 1 + 2 * odd + planes, planes)
    inside = jnp.logical_and(p > 0, p < planes - 1).astype(F32)

    def peer(k):
        return lax.rem(h + k, n)

    def rdma(src, dst, ss, rs, dev):
        return pltpu.make_async_remote_copy(
            src_ref=src, dst_ref=dst, send_sem=ss, recv_sem=rs, device_id=dev, device_id_type=MESH
        )

    def adj_copy(q):
        part = pl.ds(2 * q, 2)
        return pltpu.make_async_copy(adj_hbm.at[part], adj.at[part], adj_sem.at[q])

    for q in range(4):
        adj_copy(q).start()
    ord_copy = pltpu.make_async_copy(orders_hbm, orders, ord_sem)
    ord_copy.start()
    cond_copy = pltpu.make_async_copy(cond_hbm, cond, cond_sem)
    cond_copy.start()
    jcopy = pltpu.make_async_copy(jac_hbm, jac, jsem)
    jcopy.start()

    hx, hy = h // 2, lax.rem(h, 2)

    def at(dx, y):
        return 2 * lax.rem(hx + dx + 4, 4) + y

    def flip_dst(dx):
        return at(dx, 1 - hy)

    DIRECT = (2, 1, 3)
    FLIPS = (2, 1, 3, 0)

    barrier = pltpu.get_barrier_semaphore()
    for k in range(1, n):
        pl.semaphore_signal(barrier, inc=1, device_id=(p, peer(k)), device_id_type=MESH)
    pl.semaphore_signal(barrier, inc=1, device_id=(mate, h), device_id_type=MESH)

    for k in range(n):
        pl.semaphore_signal(barrier, inc=1, device_id=(outer, peer(k)), device_id_type=MESH)

    for q in range(4):
        adj_copy(q).wait()

        def pack(g, _, q=q):
            rows = pl.ds(pl.multiple_of(g * R, R), R)
            for i in range(3):
                both = jnp.concatenate([adj[2 * q, i, 0, rows, :], adj[2 * q + 1, i, 0, rows, :]], axis=0)
                pk[g, i, q] = both.astype(BF16)
            return 0

        lax.fori_loop(0, 2 * n, pack, 0, unroll=4)

    pl.semaphore_wait(barrier, 2 * n)

    def a2a(g, dx):
        dst = at(dx, hy)
        return rdma(pk.at[2 * dst + g], x1.at[g, :, pl.ds(4 * h, 4)], a_s.at[g, dx], a_r.at[g, dx], (p, dst))

    def a2a_flip(g, dx):
        dst = flip_dst(dx)
        return rdma(pk.at[2 * dst + g], x1.at[g, :, pl.ds(4 * h, 4)], fa_s.at[g, dx], fa_r.at[g, dx], (p, dst))

    for g in range(2):
        for dx in FLIPS:
            a2a_flip(g, dx).start()
        for dx in DIRECT:
            a2a(g, dx).start()

    for g in range(2):
        x1[g, :, pl.ds(4 * h, 4)] = pk[2 * h + g]

    ord_copy.wait()
    for k in range(H):
        mat[2 * k:2 * k + 2, :] = jnp.full((2, 128), orders[k], jnp.int32)
    steps = lax.broadcasted_iota(jnp.int32, (C, 128), 1)
    quarter = (lax.broadcasted_iota(jnp.int32, (C, 128), 0) & 1) * (NT // 4)
    phases = (mat[...] * steps + (NT - quarter)) & (NT - 1)
    tab = jnp.cos(phases.astype(F32) * (2.0 * math.pi / NT))[:, :HALF].astype(BF16)

    def iota(shape, dim):
        return lax.broadcasted_iota(jnp.int32, shape, dim)

    def spread(dims, dst):
        cols = ((iota((C, K), 1) >> 3) == iota((C, K), 0)).astype(F32).astype(BF16)
        rows = ((iota((K, C), 0) >> 3) == iota((K, C), 1)).astype(F32).astype(BF16)
        mid = lax.dot_general(rows, tab, dims, preferred_element_type=F32).astype(BF16)
        full = jnp.dot(mid, cols, preferred_element_type=F32)
        same = ((iota((K, K), 0) ^ iota((K, K), 1)) & (R - 1)) == 0
        dst[...] = jnp.where(same, full, 0.0).astype(BF16)

    spread((((1,), (1,)), ((), ())), tf)
    spread((((1,), (0,)), ((), ())), tb)

    QUARTER = 0.25

    def fill(dst, *terms):
        total = jnp.zeros(dst.shape, F32)
        for where, value in terms:
            total = jnp.where(where, value, total)
        dst[...] = total.astype(BF16)

    ya, yb = iota((128, 128), 0), iota((128, 128), 1)
    fill(my, (ya == yb, 6.0 * QUARTER), (jnp.abs(ya - yb) == 1, -QUARTER))
    sa, sb = iota((256, 256), 0), iota((256, 256), 1)
    alike = (sa >> 3) == (sb >> 3)
    fill(ms, (jnp.logical_and(alike, jnp.abs(sa - sb) == 1), -QUARTER))
    fill(mc.at[0], (jnp.logical_and(alike, sa - sb == R - 1), -QUARTER))
    fill(mc.at[1], (jnp.logical_and(alike, sb - sa == R - 1), -QUARTER))
    ha, hb = iota((256, 32), 0), iota((256, 32), 1)
    fill(mh.at[0], (ha == hb * R, -QUARTER))
    fill(mh.at[1], (ha == hb * R + R - 1, -QUARTER))
    down = sb - sa
    step_down = jnp.where((sa & (R - 1)) == R - 1, R + 1, 1)
    step_up = jnp.where((sa & (R - 1)) == 0, -(R + 1), -1)
    fill(mf, (down == step_down, -QUARTER), (down == step_up, -QUARTER))

    cond_copy.wait()
    for g in range(2):
        cnd = cond[0, pl.ds(pl.multiple_of(2 * R * h + g * R, R), R), :]
        for q in range(H):
            fac1[g, q, 0] = orders[q].astype(F32) * (1.0 / (2.0 * H)) * cnd
    for q in range(4):
        fac2[q] = (orders[4 * h + q].astype(F32) * (1.0 / (2.0 * H)) * cond[0]).reshape(2 * n, 1, R, 128)

    jcopy.wait()
    for a in range(3):
        for b in range(3):

            def fold(t, _, a=a, b=b):
                both = jac[a, b, t, 0].astype(F32) + jac[a, b, t + HALF, 0].astype(F32)
                both = both * (2.0 / NT)
                rows = pl.ds(pl.multiple_of(t * R, R), R)
                jeff[0, a, b, rows, :] = both[:R]
                jeff[1, a, b, rows, :] = both[R:]
                return 0

            lax.fori_loop(0, HALF, fold, 0, unroll=8)

    MB = 256

    def forward(src, g):
        cells = jnp.concatenate([src[g, i].reshape(K, 128) for i in range(3)], axis=1)

        def body(m, _):
            rows = pl.ds(pl.multiple_of(m * MB, MB), MB)
            smp = jnp.dot(tf[rows, :], cells, preferred_element_type=F32)
            for b in range(3):
                total = jeff[g, 0, b, rows, :] * smp[:, :128]
                total = total + jeff[g, 1, b, rows, :] * smp[:, 128:256]
                total = total + jeff[g, 2, b, rows, :] * smp[:, 256:]
                wgt[g, rows, 128 * b:128 * b + 128] = total.astype(BF16)
            return 0

        lax.fori_loop(0, K // MB, body, 0)

    def backward(g, dst, keep):
        def body(m, _):
            rows = pl.ds(pl.multiple_of(m * MB, MB), MB)
            pairs = pl.ds(m * (MB // R // 2), MB // R // 2)
            coef = jnp.dot(tb[rows, :], wgt[g], preferred_element_type=F32)
            for i in range(3):
                part = coef[:, 128 * i:128 * i + 128]
                if keep:
                    cf[i, rows, :] = part
                dst[g, i, pairs] = part.astype(BF16).reshape(MB // R // 2, 2 * R, 128)
            return 0

        lax.fori_loop(0, K // MB, body, 0)

    def xhalo(d, dst):
        return rdma(xs.at[d], xr.at[d], x_s.at[d], x_r.at[d], (p, dst))

    def zsend(g, i, d):
        if d == 0:
            return rdma(c1.at[g, i], zm.at[g, i], z_s.at[0, g, i], z_r.at[0, g, i], (mate, h))
        return rdma(c1.at[g, i], zo.at[g, i], z_s.at[1, g, i], z_r.at[1, g, i], (outer, h))

    def feed(kind, g, dx):
        dst = at(dx, hy) if kind < 2 else flip_dst(dx)
        src = (c1, zo, zo, c1)[kind]
        to = r1 if kind in (0, 2) else e1
        return rdma(
            src.at[g, :, pl.ds(4 * dst, 4)], to.at[g, h], f_s.at[kind, g, dx], f_r.at[kind, g, dx],
            (p if kind < 2 else outer, dst),
        )

    for g in range(2):
        for dx in DIRECT:
            a2a(g, dx).wait_recv()
        for dx in FLIPS:
            a2a_flip(g, dx).wait_recv()
        forward(x1, g)
        backward(g, c1, True)

        for i in range(3):
            zsend(g, i, 1).start()

        for i in range(3):
            zsend(g, i, 0).start()

        for i in range(3):
            xs[g, i] = cf[i, pl.ds(0 if g == 0 else R - 1, C, stride=R), :].astype(BF16)

        if g == 0:

            @pl.when(h > 0)
            def _():
                xhalo(0, h - 1).start()

        else:

            @pl.when(h < n - 1)
            def _():
                xhalo(1, h + 1).start()

        for dx in range(4):
            feed(3, g, dx).start()

        for dx in DIRECT:
            feed(0, g, dx).start()
        r1[g, h] = c1[g, :, pl.ds(4 * h, 4)]

    def own(g, dx):
        dst = at(dx, hy)
        return rdma(c2.at[g, :, pl.ds(4 * dst, 4)], r2.at[g, h], o_s.at[g, dx], o_r.at[g, dx], (p, dst))

    def own_flip(g, dx):
        dst = flip_dst(dx)
        return rdma(c2.at[g, :, pl.ds(4 * dst, 4)], r2.at[g, h], fc_s.at[g, dx], fc_r.at[g, dx], (p, dst))

    def edge(g, k):
        dst = peer(k)
        return rdma(c2.at[g, :, pl.ds(4 * dst, 4)], e2.at[g, h], e_s.at[g, k], e_r.at[g, k], (outer, dst))

    def to_mate(g, i):
        return rdma(r2.at[g, :, i], m2.at[g, :, i], m_s.at[g, i], m_r.at[g, i], (mate, h))

    def exchange(g):
        for dx in FLIPS:
            own_flip(g, dx).start()

        for k in (4, 5, 3, 1, 7, 2, 6, 0):
            edge(g, k).start()

        for dx in DIRECT:
            own(g, dx).start()

    def swapped(v, factor):
        return jnp.concatenate([factor * v[:, 1:], -(factor * v[:, :1])], axis=1)

    for g in range(2):
        has_x = h > 0 if g == 0 else h < n - 1

        @pl.when(has_x)
        def _():
            xhalo(1 - g, h).wait_recv()

        @pl.when(jnp.logical_not(has_x))
        def _():
            xr[1 - g] = jnp.zeros_like(xr[1 - g])

        for i in range(3):

            zsend(g, i, 1).wait_recv()

            zsend(g, i, 0).wait_recv()

            if g == 1 and i == 2:
                exchange(0)

            def first(b, _, g=g, i=i):
                pairs = pl.ds(16 * b, 16)
                mine = c1[g, i, pairs].reshape(256, 128)
                other = c1[1 - g, i, pairs].reshape(256, 128)
                halo = xr[1 - g, i, pl.ds(pl.multiple_of(32 * b, 32), 32), :]
                total = jnp.dot(mine, my[...], preferred_element_type=F32)
                total = total + jnp.dot(ms[...], mine, preferred_element_type=F32)
                total = total + jnp.dot(mc[g], other, preferred_element_type=F32)
                total = total + jnp.dot(mh[g], halo, preferred_element_type=F32)
                axial = zm[g, i, pairs].astype(F32) + inside * zo[g, i, pairs].astype(F32)
                eddy = swapped(x1[g, i, pairs].astype(F32).reshape(16, 2, R, 128), fac1[g, pairs])
                total = total.reshape(16, 2 * R, 128) - QUARTER * axial + eddy.reshape(16, 2 * R, 128)
                x2[g, i, pairs] = total.astype(BF16)
                return 0

            lax.fori_loop(0, 2, first, 0)

        for dx in range(4):
            feed(2, g, dx).start()
        for dx in DIRECT:
            feed(1, g, dx).start()
        e1[g, h] = zo[g, :, pl.ds(4 * h, 4)]

        forward(x2, g)
        backward(g, c2, False)

    exchange(1)
    for g in range(2):
        r2[g, h] = c2[g, :, pl.ds(4 * h, 4)]

    def rows(ref, i, q):
        return jnp.stack([ref[0, :, i, q], ref[1, :, i, q]], axis=1).reshape(2 * n, 2 * R, 128)

    def inplane(r, v, out, i):
        for q in range(4):
            mine = rows(r, i, q).reshape(256, 128)
            total = jnp.dot(mine, my[...], preferred_element_type=F32)
            total = total + jnp.dot(mf[...], mine, preferred_element_type=F32)
            total = total.reshape(2 * n, 2, R, 128)
            factor = fac2[q].reshape(2 * n * R, 128)
            out[2 * q, i, 0] = total[:, 0].reshape(2 * n * R, 128) + factor * v[2 * q + 1, i, 0]
            out[2 * q + 1, i, 0] = total[:, 1].reshape(2 * n * R, 128) - factor * v[2 * q, i, 0]

    def axial(e, m, out, i):
        for q in range(4):
            both = QUARTER * (inside * rows(e, i, q).astype(F32) + rows(m, i, q).astype(F32))
            both = both.reshape(2 * n, 2, R, 128)
            out[2 * q, i, 0] = out[2 * q, i, 0] - both[:, 0].reshape(2 * n * R, 128)
            out[2 * q + 1, i, 0] = out[2 * q + 1, i, 0] - both[:, 1].reshape(2 * n * R, 128)

    def first_to_mate(g):
        return rdma(r1.at[g], m1.at[g], n_s.at[g], n_r.at[g], (mate, h))

    for g in range(2):
        for dx in DIRECT:
            feed(0, g, dx).wait_recv()
        for dx in range(4):
            feed(2, g, dx).wait_recv()
        first_to_mate(g).start()

    for i in range(3):
        inplane(r1, adj, out1, i)

    for g in range(2):
        for dx in DIRECT:
            feed(1, g, dx).wait_recv()
        for dx in range(4):
            feed(3, g, dx).wait_recv()

    for g in range(2):
        first_to_mate(g).wait_recv()
    for i in range(3):
        axial(e1, m1, out1, i)

    for g in range(2):
        for dx in DIRECT:
            own(g, dx).wait_recv()
        for dx in FLIPS:
            own_flip(g, dx).wait_recv()
        for i in range(3):
            to_mate(g, i).start()
    for i in range(3):
        inplane(r2, out1, out2, i)

    for g in range(2):
        for k in range(n):
            edge(g, k).wait_recv()

    for i in range(3):
        for g in range(2):
            to_mate(g, i).wait_recv()
        axial(e2, m2, out2, i)

    for g in range(2):
        for dx in DIRECT:
            a2a(g, dx).wait_send()
            feed(0, g, dx).wait_send()
        for dx in FLIPS:
            a2a_flip(g, dx).wait_send()
        for dx in range(4):
            feed(2, g, dx).wait_send()

        for dx in DIRECT:
            feed(1, g, dx).wait_send()
        for dx in range(4):
            feed(3, g, dx).wait_send()

    @pl.when(h > 0)
    def _():
        xhalo(0, h - 1).wait_send()

    @pl.when(h < n - 1)
    def _():
        xhalo(1, h + 1).wait_send()

    for i in range(3):

        for g in range(2):
            zsend(g, i, 0).wait_send()

        for g in range(2):
            zsend(g, i, 1).wait_send()

    for g in range(2):
        first_to_mate(g).wait_send()

    for g in range(2):
        for dx in DIRECT:
            own(g, dx).wait_send()
        for dx in FLIPS:
            own_flip(g, dx).wait_send()

        for k in range(n):
            edge(g, k).wait_send()

        for i in range(3):
            to_mate(g, i).wait_send()


def shards(adjoint, jacobian, conductivity, harm_order):
    n = lax.axis_size("harm")
    hbm = pl.BlockSpec(memory_space=pltpu.HBM)
    vmem = pl.BlockSpec(memory_space=pltpu.VMEM)
    pinned = [pltpu.with_memory_space_constraint(v, pltpu.HBM) for v in (adjoint, jacobian, conductivity, harm_order)]
    shape = jax.ShapeDtypeStruct(adjoint.shape, F32)
    by_rows = (2, 3, C // 2, 2 * R, 128)
    tile = (3, C // 2 // n, 2 * R, 128)
    by_coeffs = (2, n) + tile
    dma = pltpu.SemaphoreType.DMA
    return pl.pallas_call(
        kernel,
        out_shape=(shape, shape),
        in_specs=[hbm, hbm, hbm, hbm],
        out_specs=(vmem, vmem),
        scratch_shapes=[
            pltpu.VMEM(adjoint.shape, F32),
            pltpu.VMEM(conductivity.shape, F32),
            pltpu.SMEM(harm_order.shape, jnp.int32),
            pltpu.VMEM((C, 128), jnp.int32),
            pltpu.VMEM((2 * n,) + tile, BF16),
            pltpu.VMEM(by_rows, BF16),
            pltpu.VMEM(jacobian.shape, BF16),
            pltpu.VMEM((2, 3, 3, K, 128), F32),
            pltpu.VMEM((K, K), BF16),
            pltpu.VMEM((K, K), BF16),
            pltpu.VMEM((2, K, 3 * 128), BF16),
            pltpu.VMEM((3, K, 128), F32),
            pltpu.VMEM(by_rows, BF16),
            pltpu.VMEM(by_rows, BF16),
            pltpu.VMEM(by_rows, BF16),
            pltpu.VMEM((2, 3, C, 128), BF16),
            pltpu.VMEM((2, 3, C, 128), BF16),
            pltpu.VMEM(by_rows, BF16),
            pltpu.VMEM(by_coeffs, BF16),
            pltpu.VMEM(by_coeffs, BF16),
            pltpu.VMEM(by_coeffs, BF16),
            pltpu.VMEM(by_rows, BF16),
            pltpu.VMEM(by_coeffs, BF16),
            pltpu.VMEM(by_coeffs, BF16),
            pltpu.VMEM(by_coeffs, BF16),
            pltpu.VMEM((2, H, 1, R, 128), F32),
            pltpu.VMEM((4, 2 * n, 1, R, 128), F32),
            pltpu.VMEM((128, 128), BF16),
            pltpu.VMEM((256, 256), BF16),
            pltpu.VMEM((2, 256, 256), BF16),
            pltpu.VMEM((2, 256, 32), BF16),
            pltpu.VMEM((256, 256), BF16),
            dma, dma((4,)), dma, dma,
            dma((2, n)), dma((2, n)),
            dma((2, 2, 3)), dma((2, 2, 3)),
            dma((2,)), dma((2,)),
            dma((4, 2, 4)), dma((4, 2, 4)),
            dma((2, 4)), dma((2, 4)),
            dma((2, n)), dma((2, n)),
            dma((2, 3)), dma((2, 3)),
            dma((2, 4)), dma((2, 4)),
            dma((2, 4)), dma((2, 4)),
            dma((2,)), dma((2,)),
        ],
        compiler_params=pltpu.CompilerParams(
            collective_id=0, has_side_effects=True, vmem_limit_bytes=48 * 1024 * 1024
        ),
    )(*pinned)


def solution(mesh):
    return jax.shard_map(
        shards,
        mesh=mesh,
        in_specs=(
            P("harm", None, "slab", None, None),
            P(None, None, None, "slab", "harm", None),
            P("slab", None, None),
            P(),
        ),
        out_specs=(P("harm", None, "slab", None, None), P("harm", None, "slab", None, None)),
        check_vma=False,
    )
```

```python
import math

import jax
import jax.numpy as jnp
from jax import lax
from jax.experimental import pallas as pl
from jax.experimental.pallas import tpu as pltpu
from jax.sharding import PartitionSpec as P

H = 32
NT = 128
HALF = NT // 2
C = 2 * H
R = 8
K = C * R
MESH = pl.DeviceIdType.MESH
F32 = jnp.float32
BF16 = jnp.bfloat16


def kernel(
    adj_hbm, jac_hbm, cond_hbm, orders_hbm,
    out1, out2,
    adj, cond, orders, mat, pk, x1, jac, jeff, tf, tb, wgt, cf, c1, zm, zo, xs, xr, x2, r1, e1, m1, c2, r2, e2, m2,
    fac1, fac2, my, ms, mc, mh, mf,
    jsem, adj_sem, cond_sem, ord_sem, a_s, a_r, z_s, z_r, x_s, x_r, f_s, f_r, o_s, o_r, e_s, e_r, m_s, m_r,
    fa_s, fa_r, fc_s, fc_r, n_s, n_r,
):
    p = lax.axis_index("slab")
    h = lax.axis_index("harm")
    planes = lax.axis_size("slab")
    n = lax.axis_size("harm")
    odd = lax.rem(p, 2)
    mate = p + 1 - 2 * odd
    outer = lax.rem(p - 1 + 2 * odd + planes, planes)
    inside = jnp.logical_and(p > 0, p < planes - 1).astype(F32)

    def peer(k):
        return lax.rem(h + k, n)

    def rdma(src, dst, ss, rs, dev):
        return pltpu.make_async_remote_copy(
            src_ref=src, dst_ref=dst, send_sem=ss, recv_sem=rs, device_id=dev, device_id_type=MESH
        )

    def adj_copy(q):
        part = pl.ds(2 * q, 2)
        return pltpu.make_async_copy(adj_hbm.at[part], adj.at[part], adj_sem.at[q])

    for q in range(4):
        adj_copy(q).start()
    ord_copy = pltpu.make_async_copy(orders_hbm, orders, ord_sem)
    ord_copy.start()
    cond_copy = pltpu.make_async_copy(cond_hbm, cond, cond_sem)
    cond_copy.start()
    jcopy = pltpu.make_async_copy(jac_hbm, jac, jsem)
    jcopy.start()

    hx, hy = h // 2, lax.rem(h, 2)

    def at(dx, y):
        return 2 * lax.rem(hx + dx * (1 - 2 * lax.rem(hx, 2)) + 4, 4) + y

    def flip_dst(dx):
        return at(dx, 1 - hy)

    DIRECT = (2, 1, 3)
    FLIPS = (2, 1, 3, 0)

    barrier = pltpu.get_barrier_semaphore()
    for k in range(1, n):
        pl.semaphore_signal(barrier, inc=1, device_id=(p, peer(k)), device_id_type=MESH)
    pl.semaphore_signal(barrier, inc=1, device_id=(mate, h), device_id_type=MESH)

    for k in range(n):
        pl.semaphore_signal(barrier, inc=1, device_id=(outer, peer(k)), device_id_type=MESH)

    for q in range(4):
        adj_copy(q).wait()

        def pack(g, _, q=q):
            rows = pl.ds(pl.multiple_of(g * R, R), R)
            for i in range(3):
                both = jnp.concatenate([adj[2 * q, i, 0, rows, :], adj[2 * q + 1, i, 0, rows, :]], axis=0)
                pk[g, i, q] = both.astype(BF16)
            return 0

        lax.fori_loop(0, 2 * n, pack, 0, unroll=4)

    pl.semaphore_wait(barrier, 2 * n)

    def a2a(g, dx):
        dst = at(dx, hy)
        return rdma(pk.at[2 * dst + g], x1.at[g, :, pl.ds(4 * h, 4)], a_s.at[g, dx], a_r.at[g, dx], (p, dst))

    def a2a_flip(g, dx):
        dst = flip_dst(dx)
        return rdma(pk.at[2 * dst + g], x1.at[g, :, pl.ds(4 * h, 4)], fa_s.at[g, dx], fa_r.at[g, dx], (p, dst))

    for g in range(2):
        for dx in FLIPS:
            a2a_flip(g, dx).start()
        for dx in DIRECT:
            a2a(g, dx).start()

    for g in range(2):
        x1[g, :, pl.ds(4 * h, 4)] = pk[2 * h + g]

    ord_copy.wait()
    for k in range(H):
        mat[2 * k:2 * k + 2, :] = jnp.full((2, 128), orders[k], jnp.int32)
    steps = lax.broadcasted_iota(jnp.int32, (C, 128), 1)
    quarter = (lax.broadcasted_iota(jnp.int32, (C, 128), 0) & 1) * (NT // 4)
    phases = (mat[...] * steps + (NT - quarter)) & (NT - 1)
    tab = jnp.cos(phases.astype(F32) * (2.0 * math.pi / NT))[:, :HALF].astype(BF16)

    def iota(shape, dim):
        return lax.broadcasted_iota(jnp.int32, shape, dim)

    def spread(dims, dst):
        cols = ((iota((C, K), 1) >> 3) == iota((C, K), 0)).astype(F32).astype(BF16)
        rows = ((iota((K, C), 0) >> 3) == iota((K, C), 1)).astype(F32).astype(BF16)
        mid = lax.dot_general(rows, tab, dims, preferred_element_type=F32).astype(BF16)
        full = jnp.dot(mid, cols, preferred_element_type=F32)
        same = ((iota((K, K), 0) ^ iota((K, K), 1)) & (R - 1)) == 0
        dst[...] = jnp.where(same, full, 0.0).astype(BF16)

    spread((((1,), (1,)), ((), ())), tf)
    spread((((1,), (0,)), ((), ())), tb)

    QUARTER = 0.25

    def fill(dst, *terms):
        total = jnp.zeros(dst.shape, F32)
        for where, value in terms:
            total = jnp.where(where, value, total)
        dst[...] = total.astype(BF16)

    ya, yb = iota((128, 128), 0), iota((128, 128), 1)
    fill(my, (ya == yb, 6.0 * QUARTER), (jnp.abs(ya - yb) == 1, -QUARTER))
    sa, sb = iota((256, 256), 0), iota((256, 256), 1)
    alike = (sa >> 3) == (sb >> 3)
    fill(ms, (jnp.logical_and(alike, jnp.abs(sa - sb) == 1), -QUARTER))
    fill(mc.at[0], (jnp.logical_and(alike, sa - sb == R - 1), -QUARTER))
    fill(mc.at[1], (jnp.logical_and(alike, sb - sa == R - 1), -QUARTER))
    ha, hb = iota((256, 32), 0), iota((256, 32), 1)
    fill(mh.at[0], (ha == hb * R, -QUARTER))
    fill(mh.at[1], (ha == hb * R + R - 1, -QUARTER))
    down = sb - sa
    step_down = jnp.where((sa & (R - 1)) == R - 1, R + 1, 1)
    step_up = jnp.where((sa & (R - 1)) == 0, -(R + 1), -1)
    fill(mf, (down == step_down, -QUARTER), (down == step_up, -QUARTER))

    cond_copy.wait()
    for g in range(2):
        cnd = cond[0, pl.ds(pl.multiple_of(2 * R * h + g * R, R), R), :]
        for q in range(H):
            fac1[g, q, 0] = orders[q].astype(F32) * (1.0 / (2.0 * H)) * cnd
    for q in range(4):
        fac2[q] = (orders[4 * h + q].astype(F32) * (1.0 / (2.0 * H)) * cond[0]).reshape(2 * n, 1, R, 128)

    jcopy.wait()
    for a in range(3):
        for b in range(3):

            def fold(t, _, a=a, b=b):
                both = jac[a, b, t, 0].astype(F32) + jac[a, b, t + HALF, 0].astype(F32)
                both = both * (2.0 / NT)
                rows = pl.ds(pl.multiple_of(t * R, R), R)
                jeff[0, a, b, rows, :] = both[:R]
                jeff[1, a, b, rows, :] = both[R:]
                return 0

            lax.fori_loop(0, HALF, fold, 0, unroll=8)

    MB = 256

    def forward(src, g):
        cells = jnp.concatenate([src[g, i].reshape(K, 128) for i in range(3)], axis=1)

        def body(m, _):
            rows = pl.ds(pl.multiple_of(m * MB, MB), MB)
            smp = jnp.dot(tf[rows, :], cells, preferred_element_type=F32)
            for b in range(3):
                total = jeff[g, 0, b, rows, :] * smp[:, :128]
                total = total + jeff[g, 1, b, rows, :] * smp[:, 128:256]
                total = total + jeff[g, 2, b, rows, :] * smp[:, 256:]
                wgt[g, rows, 128 * b:128 * b + 128] = total.astype(BF16)
            return 0

        lax.fori_loop(0, K // MB, body, 0)

    def backward(g, dst, keep):
        def body(m, _):
            rows = pl.ds(pl.multiple_of(m * MB, MB), MB)
            pairs = pl.ds(m * (MB // R // 2), MB // R // 2)
            coef = jnp.dot(tb[rows, :], wgt[g], preferred_element_type=F32)
            for i in range(3):
                part = coef[:, 128 * i:128 * i + 128]
                if keep:
                    cf[i, rows, :] = part
                dst[g, i, pairs] = part.astype(BF16).reshape(MB // R // 2, 2 * R, 128)
            return 0

        lax.fori_loop(0, K // MB, body, 0)

    def xhalo(d, dst):
        return rdma(xs.at[d], xr.at[d], x_s.at[d], x_r.at[d], (p, dst))

    def zsend(g, i, d):
        if d == 0:
            return rdma(c1.at[g, i], zm.at[g, i], z_s.at[0, g, i], z_r.at[0, g, i], (mate, h))
        return rdma(c1.at[g, i], zo.at[g, i], z_s.at[1, g, i], z_r.at[1, g, i], (outer, h))

    def feed(kind, g, dx):
        dst = at(dx, hy) if kind < 2 else flip_dst(dx)
        src = (c1, zo, zo, c1)[kind]
        to = r1 if kind in (0, 2) else e1
        return rdma(
            src.at[g, :, pl.ds(4 * dst, 4)], to.at[g, h], f_s.at[kind, g, dx], f_r.at[kind, g, dx],
            (p if kind < 2 else outer, dst),
        )

    for g in range(2):
        for dx in DIRECT:
            a2a(g, dx).wait_recv()
        for dx in FLIPS:
            a2a_flip(g, dx).wait_recv()
        forward(x1, g)
        backward(g, c1, True)

        for i in range(3):
            zsend(g, i, 1).start()

        for i in range(3):
            zsend(g, i, 0).start()

        for i in range(3):
            xs[g, i] = cf[i, pl.ds(0 if g == 0 else R - 1, C, stride=R), :].astype(BF16)

        if g == 0:

            @pl.when(h > 0)
            def _():
                xhalo(0, h - 1).start()

        else:

            @pl.when(h < n - 1)
            def _():
                xhalo(1, h + 1).start()

        for dx in range(4):
            feed(3, g, dx).start()

        for dx in DIRECT:
            feed(0, g, dx).start()
        r1[g, h] = c1[g, :, pl.ds(4 * h, 4)]

    def own(g, dx):
        dst = at(dx, hy)
        return rdma(c2.at[g, :, pl.ds(4 * dst, 4)], r2.at[g, h], o_s.at[g, dx], o_r.at[g, dx], (p, dst))

    def own_flip(g, dx):
        dst = flip_dst(dx)
        return rdma(c2.at[g, :, pl.ds(4 * dst, 4)], r2.at[g, h], fc_s.at[g, dx], fc_r.at[g, dx], (p, dst))

    def edge(g, k):
        dst = peer(k)
        return rdma(c2.at[g, :, pl.ds(4 * dst, 4)], e2.at[g, h], e_s.at[g, k], e_r.at[g, k], (outer, dst))

    def to_mate(g, i):
        return rdma(r2.at[g, :, i], m2.at[g, :, i], m_s.at[g, i], m_r.at[g, i], (mate, h))

    def exchange(g):
        for dx in FLIPS:
            own_flip(g, dx).start()

        for k in (4, 5, 3, 1, 7, 2, 6, 0):
            edge(g, k).start()

        for dx in DIRECT:
            own(g, dx).start()

    def swapped(v, factor):
        return jnp.concatenate([factor * v[:, 1:], -(factor * v[:, :1])], axis=1)

    for g in range(2):
        has_x = h > 0 if g == 0 else h < n - 1

        @pl.when(has_x)
        def _():
            xhalo(1 - g, h).wait_recv()

        @pl.when(jnp.logical_not(has_x))
        def _():
            xr[1 - g] = jnp.zeros_like(xr[1 - g])

        for i in range(3):

            zsend(g, i, 1).wait_recv()

            zsend(g, i, 0).wait_recv()

            if g == 1 and i == 2:
                exchange(0)

            def first(b, _, g=g, i=i):
                pairs = pl.ds(16 * b, 16)
                mine = c1[g, i, pairs].reshape(256, 128)
                other = c1[1 - g, i, pairs].reshape(256, 128)
                halo = xr[1 - g, i, pl.ds(pl.multiple_of(32 * b, 32), 32), :]
                total = jnp.dot(mine, my[...], preferred_element_type=F32)
                total = total + jnp.dot(ms[...], mine, preferred_element_type=F32)
                total = total + jnp.dot(mc[g], other, preferred_element_type=F32)
                total = total + jnp.dot(mh[g], halo, preferred_element_type=F32)
                axial = zm[g, i, pairs].astype(F32) + inside * zo[g, i, pairs].astype(F32)
                eddy = swapped(x1[g, i, pairs].astype(F32).reshape(16, 2, R, 128), fac1[g, pairs])
                total = total.reshape(16, 2 * R, 128) - QUARTER * axial + eddy.reshape(16, 2 * R, 128)
                x2[g, i, pairs] = total.astype(BF16)
                return 0

            lax.fori_loop(0, 2, first, 0)

        for dx in range(4):
            feed(2, g, dx).start()
        for dx in DIRECT:
            feed(1, g, dx).start()
        e1[g, h] = zo[g, :, pl.ds(4 * h, 4)]

        forward(x2, g)
        backward(g, c2, False)

    exchange(1)
    for g in range(2):
        r2[g, h] = c2[g, :, pl.ds(4 * h, 4)]

    def rows(ref, i, q):
        return jnp.stack([ref[0, :, i, q], ref[1, :, i, q]], axis=1).reshape(2 * n, 2 * R, 128)

    def inplane(r, v, out, i):
        for q in range(4):
            mine = rows(r, i, q).reshape(256, 128)
            total = jnp.dot(mine, my[...], preferred_element_type=F32)
            total = total + jnp.dot(mf[...], mine, preferred_element_type=F32)
            total = total.reshape(2 * n, 2, R, 128)
            factor = fac2[q].reshape(2 * n * R, 128)
            out[2 * q, i, 0] = total[:, 0].reshape(2 * n * R, 128) + factor * v[2 * q + 1, i, 0]
            out[2 * q + 1, i, 0] = total[:, 1].reshape(2 * n * R, 128) - factor * v[2 * q, i, 0]

    def axial(e, m, out, i):
        for q in range(4):
            both = QUARTER * (inside * rows(e, i, q).astype(F32) + rows(m, i, q).astype(F32))
            both = both.reshape(2 * n, 2, R, 128)
            out[2 * q, i, 0] = out[2 * q, i, 0] - both[:, 0].reshape(2 * n * R, 128)
            out[2 * q + 1, i, 0] = out[2 * q + 1, i, 0] - both[:, 1].reshape(2 * n * R, 128)

    def first_to_mate(g):
        return rdma(r1.at[g], m1.at[g], n_s.at[g], n_r.at[g], (mate, h))

    for g in range(2):
        for dx in DIRECT:
            feed(0, g, dx).wait_recv()
        for dx in range(4):
            feed(2, g, dx).wait_recv()
        first_to_mate(g).start()

    for i in range(3):
        inplane(r1, adj, out1, i)

    for g in range(2):
        for dx in DIRECT:
            feed(1, g, dx).wait_recv()
        for dx in range(4):
            feed(3, g, dx).wait_recv()

    for g in range(2):
        first_to_mate(g).wait_recv()
    for i in range(3):
        axial(e1, m1, out1, i)

    for g in range(2):
        for dx in DIRECT:
            own(g, dx).wait_recv()
        for dx in FLIPS:
            own_flip(g, dx).wait_recv()
        for i in range(3):
            to_mate(g, i).start()
    for i in range(3):
        inplane(r2, out1, out2, i)

    for g in range(2):
        for k in range(n):
            edge(g, k).wait_recv()

    for i in range(3):
        for g in range(2):
            to_mate(g, i).wait_recv()
        axial(e2, m2, out2, i)

    for g in range(2):
        for dx in DIRECT:
            a2a(g, dx).wait_send()
            feed(0, g, dx).wait_send()
        for dx in FLIPS:
            a2a_flip(g, dx).wait_send()
        for dx in range(4):
            feed(2, g, dx).wait_send()

        for dx in DIRECT:
            feed(1, g, dx).wait_send()
        for dx in range(4):
            feed(3, g, dx).wait_send()

    @pl.when(h > 0)
    def _():
        xhalo(0, h - 1).wait_send()

    @pl.when(h < n - 1)
    def _():
        xhalo(1, h + 1).wait_send()

    for i in range(3):

        for g in range(2):
            zsend(g, i, 0).wait_send()

        for g in range(2):
            zsend(g, i, 1).wait_send()

    for g in range(2):
        first_to_mate(g).wait_send()

    for g in range(2):
        for dx in DIRECT:
            own(g, dx).wait_send()
        for dx in FLIPS:
            own_flip(g, dx).wait_send()

        for k in range(n):
            edge(g, k).wait_send()

        for i in range(3):
            to_mate(g, i).wait_send()


def shards(adjoint, jacobian, conductivity, harm_order):
    n = lax.axis_size("harm")
    hbm = pl.BlockSpec(memory_space=pltpu.HBM)
    vmem = pl.BlockSpec(memory_space=pltpu.VMEM)
    pinned = [pltpu.with_memory_space_constraint(v, pltpu.HBM) for v in (adjoint, jacobian, conductivity, harm_order)]
    shape = jax.ShapeDtypeStruct(adjoint.shape, F32)
    by_rows = (2, 3, C // 2, 2 * R, 128)
    tile = (3, C // 2 // n, 2 * R, 128)
    by_coeffs = (2, n) + tile
    dma = pltpu.SemaphoreType.DMA
    return pl.pallas_call(
        kernel,
        out_shape=(shape, shape),
        in_specs=[hbm, hbm, hbm, hbm],
        out_specs=(vmem, vmem),
        scratch_shapes=[
            pltpu.VMEM(adjoint.shape, F32),
            pltpu.VMEM(conductivity.shape, F32),
            pltpu.SMEM(harm_order.shape, jnp.int32),
            pltpu.VMEM((C, 128), jnp.int32),
            pltpu.VMEM((2 * n,) + tile, BF16),
            pltpu.VMEM(by_rows, BF16),
            pltpu.VMEM(jacobian.shape, BF16),
            pltpu.VMEM((2, 3, 3, K, 128), F32),
            pltpu.VMEM((K, K), BF16),
            pltpu.VMEM((K, K), BF16),
            pltpu.VMEM((2, K, 3 * 128), BF16),
            pltpu.VMEM((3, K, 128), F32),
            pltpu.VMEM(by_rows, BF16),
            pltpu.VMEM(by_rows, BF16),
            pltpu.VMEM(by_rows, BF16),
            pltpu.VMEM((2, 3, C, 128), BF16),
            pltpu.VMEM((2, 3, C, 128), BF16),
            pltpu.VMEM(by_rows, BF16),
            pltpu.VMEM(by_coeffs, BF16),
            pltpu.VMEM(by_coeffs, BF16),
            pltpu.VMEM(by_coeffs, BF16),
            pltpu.VMEM(by_rows, BF16),
            pltpu.VMEM(by_coeffs, BF16),
            pltpu.VMEM(by_coeffs, BF16),
            pltpu.VMEM(by_coeffs, BF16),
            pltpu.VMEM((2, H, 1, R, 128), F32),
            pltpu.VMEM((4, 2 * n, 1, R, 128), F32),
            pltpu.VMEM((128, 128), BF16),
            pltpu.VMEM((256, 256), BF16),
            pltpu.VMEM((2, 256, 256), BF16),
            pltpu.VMEM((2, 256, 32), BF16),
            pltpu.VMEM((256, 256), BF16),
            dma, dma((4,)), dma, dma,
            dma((2, n)), dma((2, n)),
            dma((2, 2, 3)), dma((2, 2, 3)),
            dma((2,)), dma((2,)),
            dma((4, 2, 4)), dma((4, 2, 4)),
            dma((2, 4)), dma((2, 4)),
            dma((2, n)), dma((2, n)),
            dma((2, 3)), dma((2, 3)),
            dma((2, 4)), dma((2, 4)),
            dma((2, 4)), dma((2, 4)),
            dma((2,)), dma((2,)),
        ],
        compiler_params=pltpu.CompilerParams(
            collective_id=0, has_side_effects=True, vmem_limit_bytes=48 * 1024 * 1024
        ),
    )(*pinned)


def solution(mesh):
    return jax.shard_map(
        shards,
        mesh=mesh,
        in_specs=(
            P("harm", None, "slab", None, None),
            P(None, None, None, "slab", "harm", None),
            P("slab", None, None),
            P(),
        ),
        out_specs=(P("harm", None, "slab", None, None), P("harm", None, "slab", None, None)),
        check_vma=False,
    )
```
